512 devices in a mesh: band: 16 (over y, x_lo, core), tmpl: 32 (over z, x_hi).
Axes of the slice: x: 4 (x_hi: 2, x_lo: 2; x = x_hi * 2 + x_lo), y: 4, z: 16, core: 2. Of those that a mesh axis runs over, the one named last changes fastest.
Arguments:
- templates: float32 [2, 2048, 65536], P(None, 'tmpl', 'band'), may hold values from -100 to 100
Outputs:
- moduli: float32 [2048, 5, 64], P('tmpl')
The draws below stay inside these ranges and needn't reach their ends.
All inputs are finite; a program needn't handle non-finite values.
Results may differ from the reference program's by a relative error of at most 0.0003.
Values sent between devices are 32-bit elements; how exact they have to be, the bound alone decides.
No kernel may reach another device: no remote copies, remote signals or barrier semaphores. Data moves between devices by JAX's collectives and lax.ppermute only.
A program may use at most 64 MiB of HBM per device.

```python
import math
import jax
import jax.numpy as jnp
from jax import lax

TB = 64
F = 65536
ROUNDS = 4
TEMPLATES = 2048
N_TMPL = 32


def draw_templates(key, part):
    key = jax.random.fold_in(key, 7)
    key_scale, key_order, key_delay, key_offset, key_weight, key_rough = jax.random.split(key, 6)
    position = jnp.arange(F, dtype=jnp.float32) / F
    frequency = 1.0 + position
    ordering = (jnp.arange(TEMPLATES, dtype=jnp.float32)[:, None] + jax.random.uniform(key_order, (TEMPLATES, 1), dtype=jnp.float32, minval=-2.0, maxval=2.0)) / TEMPLATES
    chirp_cycles = 120.0 * (1.0 + 1.5 * ordering)
    delay_cycles = jax.random.uniform(key_delay, (TEMPLATES, 1), dtype=jnp.float32, minval=0.0, maxval=2.0)
    offset = jax.random.uniform(key_offset, (TEMPLATES, 1), dtype=jnp.float32) * (2.0 * math.pi)
    scale_factor = jnp.exp(jax.random.uniform(key_scale, (TEMPLATES, 1), dtype=jnp.float32, minval=math.log(0.25), maxval=math.log(2.5)))
    whitening = 12.0 * jnp.exp(0.6 * jax.random.truncated_normal(key_weight, -2.5, 2.5, (1, F), dtype=jnp.float32) - 1.5)
    rough_factor = 1.0 + 0.5 * jax.random.truncated_normal(key_rough, -4.0, 4.0, (TEMPLATES, F), dtype=jnp.float32)
    amplitude = scale_factor * frequency[None, :] ** (-7.0 / 6.0) * whitening * rough_factor
    cycles = delay_cycles * position[None, :] + chirp_cycles * (frequency[None, :] ** (-5.0 / 3.0) - 1.0)
    phase_angle = 2.0 * math.pi * cycles + offset
    return jnp.stack([amplitude * jnp.cos(phase_angle), amplitude * jnp.sin(phase_angle)]).astype(jnp.float32)


def setup_inputs(seed: int = 0) -> dict:
    key_of = jax.random.split(jax.random.key(seed), 2)
    return {
        "templates": draw_templates(jax.random.fold_in(key_of[1], 71), 0),
    }


def pair_tile(left_block, right_block):
    width = left_block.shape[1]
    left_rows = left_block.reshape(2 * width, left_block.shape[2])
    right_rows = right_block.reshape(2 * width, right_block.shape[2])
    products = lax.dot_general(left_rows, right_rows, (((1,), (1,)), ((), ())), precision=lax.Precision.HIGHEST, preferred_element_type=jnp.float32).reshape(2, width, 2, width)
    real_part = products[0, :, 0] + products[1, :, 1]
    imag_part = products[0, :, 1] - products[1, :, 0]
    return jnp.stack([real_part, imag_part])

def reference(templates):
    energy = lax.optimization_barrier(jnp.sum(templates * templates, axis=(0, 2)))
    normed = templates / jnp.sqrt(energy + 1e-06)[None, :, None]

    def one_block(index):
        left_block = lax.dynamic_slice_in_dim(normed, (index * TB).astype(jnp.int32), TB, 1)
        tiles = []
        for offset in range(ROUNDS + 1):
            partner_index = jnp.bitwise_xor(index, jnp.int32(offset)).astype(jnp.int32)
            right_block = lax.dynamic_slice_in_dim(normed, (partner_index * TB).astype(jnp.int32), TB, 1)
            tiles.append(pair_tile(left_block, right_block))
        stacked = jnp.stack(tiles, axis=2)
        return jnp.sqrt(stacked[0] * stacked[0] + stacked[1] * stacked[1])
    blocks = lax.map(one_block, jnp.arange(N_TMPL, dtype=jnp.int32))
    return blocks.reshape(TEMPLATES, ROUNDS + 1, TB)
```

```python
import jax
import jax.numpy as jnp
from jax import lax
from jax.experimental import pallas as pl
from jax.experimental.pallas import tpu as pltpu
from jax.sharding import Mesh, PartitionSpec as P

BAND = ("y", "x_lo", "core")
QUAD = ("z0", "x_hi")
TMPL = ("z_hi", "z1", "z0", "x_hi")
SCALE = 2.0**30
EPSILON = 1e-06 * 2.0**60
RELAYED = True
VMEM = pl.BlockSpec(memory_space=pltpu.VMEM)


def call(kernel, shapes, *args):
    return pl.pallas_call(
        kernel,
        out_shape=shapes,
        in_specs=[VMEM] * len(args),
        out_specs=jax.tree.map(lambda _: VMEM, shapes),
        compiler_params=pltpu.CompilerParams(vmem_limit_bytes=48 * 2**20),
    )(*args)


def f32(*shape):
    return jax.ShapeDtypeStruct(shape, jnp.float32)


def split(value):
    scaled = value * SCALE
    high = scaled.astype(jnp.bfloat16)
    low = (scaled - high.astype(jnp.float32)).astype(jnp.bfloat16)
    return high, low


def dot(left, right):
    return lax.dot_general(left, right, (((1,), (1,)), ((), ())), preferred_element_type=jnp.float32)


def complex_tile(products):
    lane = lax.broadcasted_iota(jnp.int32, (64, 128), 1)
    crossed = pltpu.roll(products[64:], 64, axis=1)
    return products[:64] + jnp.where(lane < 64, crossed, -crossed)


def modulus(tile):
    real_part = jnp.abs(tile[:, :64])
    imag_part = jnp.abs(tile[:, 64:])
    large = jnp.maximum(real_part, imag_part)
    small = jnp.minimum(real_part, imag_part)
    ratio = small / jnp.where(large > 0, large, 1.0)
    return large * jnp.sqrt(1.0 + ratio * ratio)


def quad_kernel(blocks_ref, out_ref):
    rows = blocks_ref[...].reshape(512, 1024)
    high, low = split(rows)
    products = dot(high, high) + dot(high, low) + dot(low, high)
    for a in range(4):
        for k in range(4):
            b = a ^ k
            tile = complex_tile(products[128 * a : 128 * a + 128, 128 * b : 128 * b + 128])
            at = a * 16 + (k % 2) * 8
            for group in range(8):
                out_ref[2 * group + k // 2, at : at + 8, :] = tile[8 * group : 8 * group + 8]


def far_kernel(own_ref, far_ref, energy_ref, keep_ref, send_ref):
    own = jnp.concatenate(split(own_ref[...].reshape(128, 2048)), axis=0)
    far = jnp.concatenate(split(far_ref[...].reshape(128, 2048)), axis=0)
    passes = dot(own, far)
    products = passes[:128, :128] + (passes[:128, 128:] + passes[128:, :128]) + passes[128:, 128:]
    keep_ref[...] = complex_tile(products)
    send_ref[:64, :] = complex_tile(products.T)
    send_ref[64:, :] = energy_ref[...]


def pack_kernel(quad_ref, keep_ref, got_ref, out_ref):
    far_tile = keep_ref[...] + got_ref[:64, :]
    near = quad_ref[0, :16] + quad_ref[1, :16] + quad_ref[2, :16] + quad_ref[3, :16]
    near = jnp.concatenate([modulus(near[:8]), modulus(near[8:])], axis=1)
    for place in range(16):
        out_ref[place, :64, :] = far_tile
        out_ref[place, 64:72, :] = near
        for source in range(4):
            out_ref[place, 72 + source : 73 + source, :] = quad_ref[source, 16:17, :]
        out_ref[place, 76:80, :] = got_ref[64:68, :]


def final_kernel(member_ref, shares_ref, out_ref):
    member = member_ref[0]
    far_tile = shares_ref[0, :64, :]
    energies = shares_ref[0, 72:80, :]
    for place in range(1, 16):
        far_tile = far_tile + shares_ref[place, :64, :]
        energies = energies + shares_ref[place, 72:80, :]
    inverse = (1.0 / jnp.sqrt(energies + EPSILON))[:, :64]
    row = lax.broadcasted_iota(jnp.int32, (8, 64), 0)
    columns = [jnp.sum(jnp.where(row == (member ^ k), inverse, 0.0), axis=0, keepdims=True) for k in range(4)]
    columns.append(inverse[4:5])
    diagonal = lax.broadcasted_iota(jnp.int32, (64, 64), 0) == lax.broadcasted_iota(jnp.int32, (64, 64), 1)
    own = jnp.sum(jnp.where(diagonal, columns[0], 0.0), axis=1, keepdims=True)
    for k in range(5):
        if k < 4:
            at = (k % 2) * 64
            near = [shares_ref[2 * group + k // 2, 64:72, at : at + 64] for group in range(8)]
            tile = jnp.concatenate(near, axis=0)
        else:
            tile = modulus(far_tile)
        out_ref[k] = tile * own * columns[k]


def local(templates):
    z = 2 * lax.axis_index("z1") + lax.axis_index("z0")
    member = 2 * lax.axis_index("z0") + lax.axis_index("x_hi")
    own_half = lax.axis_index("z1")
    outgoing = lax.dynamic_slice_in_dim(templates, (1 - own_half) * 2048, 2048, 2)
    if RELAYED:
        passing = lax.ppermute(outgoing, ("z1", "z0"), [(1, 2), (2, 1)])
    outgoing, templates = lax.optimization_barrier((outgoing, templates))
    quarters = templates.reshape(2, 64, 4, 1024).transpose(2, 0, 1, 3)
    quad = lax.all_to_all(quarters, QUAD, 0, 0)
    if RELAYED:
        onward = jnp.where((z == 1) | (z == 2), passing, outgoing)
        far = lax.ppermute(onward, ("z1", "z0"), [(0, 2), (3, 1), (2, 3), (1, 0)])
    else:
        far = lax.ppermute(outgoing, "z1", [(0, 1), (1, 0)])
    scaled = templates * SCALE
    energy = jnp.sum(scaled * scaled, axis=(0, 2))
    energy_rows = jnp.zeros((8, 128), jnp.float32).at[0, :64].set(energy)
    own = lax.dynamic_slice_in_dim(templates, own_half * 2048, 2048, 2)

    spread = lax.all_to_all(call(quad_kernel, f32(16, 64, 128), quad), BAND, 0, 0)
    summed = jnp.sum(spread, axis=0).reshape(4, 16, 128)
    to_quad = jnp.concatenate([summed, jnp.broadcast_to(energy_rows, (4, 8, 128))], axis=1)
    from_quad = lax.all_to_all(to_quad, QUAD, 0, 0)

    keep, send = call(far_kernel, (f32(64, 128), f32(72, 128)), own, far, energy_rows)
    got = lax.ppermute(send, "z1", [(0, 1), (1, 0)])
    shares = call(pack_kernel, f32(16, 80, 128), from_quad, keep, got)
    gathered = lax.all_to_all(shares, BAND, 0, 0)
    by_offset = pl.pallas_call(
        final_kernel,
        out_shape=f32(5, 64, 64),
        in_specs=[pl.BlockSpec(memory_space=pltpu.SMEM), VMEM],
        out_specs=VMEM,
        compiler_params=pltpu.CompilerParams(vmem_limit_bytes=48 * 2**20),
    )(member.astype(jnp.int32).reshape(1), gathered)
    return by_offset.transpose(1, 0, 2)


def solution(mesh):
    devices = mesh.devices.reshape(4, 2, 2, 4, 2, 2, 2)
    finer = Mesh(devices, ("y", "x_lo", "core", "z_hi", "z1", "z0", "x_hi"))
    in_specs = (P(None, TMPL, BAND),)
    out_specs = P(TMPL, None, None)
    return jax.shard_map(local, mesh=finer, in_specs=in_specs, out_specs=out_specs, check_vma=False)
```

```python
import functools

import jax
import jax.numpy as jnp
from jax import lax
from jax.experimental import pallas as pl
from jax.experimental.pallas import tpu as pltpu
from jax.sharding import Mesh, PartitionSpec as P

BAND = ("y", "x_lo", "core")
QUAD = ("z0", "x_hi")
FAR = ("z1", "x_lo", "core")
TMPL = ("z_hi", "z1", "z0", "x_hi")
SCALE = 2.0**30
EPSILON = 1e-06 * 2.0**60
VMEM = pl.BlockSpec(memory_space=pltpu.VMEM)
HBM = pl.BlockSpec(memory_space=pltpu.HBM)


def call(kernel, shapes, *args):
    return pl.pallas_call(
        kernel,
        out_shape=shapes,
        in_specs=[VMEM] * len(args),
        out_specs=jax.tree.map(lambda _: VMEM, shapes),
        compiler_params=pltpu.CompilerParams(vmem_limit_bytes=16 * 2**20),
    )(*args)


def f32(*shape):
    return jax.ShapeDtypeStruct(shape, jnp.float32)


def split(value):
    scaled = value * SCALE
    high = scaled.astype(jnp.bfloat16)
    low = (scaled - high.astype(jnp.float32)).astype(jnp.bfloat16)
    return high, low


def dot(left, right):
    return lax.dot_general(left, right, (((1,), (1,)), ((), ())), preferred_element_type=jnp.float32)


def complex_tile(products):
    lane = lax.broadcasted_iota(jnp.int32, (64, 128), 1)
    crossed = pltpu.roll(products[64:], 64, axis=1)
    return products[:64] + jnp.where(lane < 64, crossed, -crossed)


def modulus(tile):
    real_part = jnp.abs(tile[:, :64])
    imag_part = jnp.abs(tile[:, 64:])
    large = jnp.maximum(real_part, imag_part)
    small = jnp.minimum(real_part, imag_part)
    ratio = small / jnp.where(large > 0, large, 1.0)
    return large * jnp.sqrt(1.0 + ratio * ratio)


def member_index():
    return 2 * lax.axis_index("z0") + lax.axis_index("x_hi")


def is_middle():
    return lax.axis_index("z1") != lax.axis_index("z0")


def half_kernel(at, templates_ref, out_ref, sem):
    copy = pltpu.make_async_copy(templates_ref.at[:, :, at : at + 2048], out_ref, sem)
    copy.start()
    copy.wait()


def half(templates, at):
    return pl.pallas_call(
        functools.partial(half_kernel, at),
        out_shape=f32(2, 64, 2048),
        in_specs=[HBM],
        out_specs=VMEM,
        scratch_shapes=[pltpu.SemaphoreType.DMA],
        compiler_params=pltpu.CompilerParams(vmem_limit_bytes=8 * 2**20),
    )(templates)


def quarters_kernel(offsets, templates_ref, *refs):
    copies = []
    for place, offset in enumerate(offsets):
        at = pl.multiple_of((member_index() ^ offset) * 1024, 1024)
        copies.append(pltpu.make_async_copy(templates_ref.at[:, :, pl.ds(at, 1024)], refs[place], refs[-1].at[place]))
    for copy in copies:
        copy.start()
    for copy in copies:
        copy.wait()


def quarters(templates, *offsets):
    return pl.pallas_call(
        functools.partial(quarters_kernel, offsets),
        out_shape=(f32(2, 64, 1024),) * len(offsets),
        in_specs=[HBM],
        out_specs=(VMEM,) * len(offsets),
        scratch_shapes=[pltpu.SemaphoreType.DMA((len(offsets),))],
        compiler_params=pltpu.CompilerParams(vmem_limit_bytes=8 * 2**20),
    )(templates)


def choose_kernel(second_ref, passing_ref, out_ref, sem):
    @pl.when(is_middle())
    def _():
        copy = pltpu.make_async_copy(passing_ref, out_ref, sem)
        copy.start()
        copy.wait()

    @pl.when(jnp.logical_not(is_middle()))
    def _():
        copy = pltpu.make_async_copy(second_ref, out_ref, sem)
        copy.start()
        copy.wait()


def choose(second, passing):
    return pl.pallas_call(
        choose_kernel,
        out_shape=f32(2, 64, 2048),
        in_specs=[VMEM] * 2,
        out_specs=VMEM,
        scratch_shapes=[pltpu.SemaphoreType.DMA],
        compiler_params=pltpu.CompilerParams(vmem_limit_bytes=8 * 2**20),
    )(second, passing)


def row_of(column):
    row = lax.broadcasted_iota(jnp.int32, (64, 128), 0)
    lane = lax.broadcasted_iota(jnp.int32, (64, 128), 1)
    return jnp.sum(jnp.where(row == lane, column, 0.0), axis=0, keepdims=True)


def own_kernel(templates_ref, own_ref, energy_ref):
    at = pl.multiple_of(jnp.where(is_middle(), 2048, 0), 2048)
    high, low = split(templates_ref[:, :, pl.ds(at, 2048)].reshape(128, 2048))
    own_ref[:128, :] = high
    own_ref[128:, :] = low
    squares = jnp.zeros((64, 128), jnp.float32)
    for start in range(0, 4096, 128):
        for part in range(2):
            values = templates_ref[part, :, start : start + 128] * SCALE
            squares = squares + values * values
    energy_ref[...] = jnp.zeros((8, 128), jnp.float32)
    energy_ref[:1, :] = row_of(jnp.sum(squares, axis=1, keepdims=True))


def near_kernel(own_ref, three_ref, two_ref, one_ref, out_ref):
    blocks = [own_ref[...], one_ref[...], two_ref[...], three_ref[...]]
    rows = jnp.concatenate([block.reshape(128, 1024) for block in blocks], axis=0)
    high, low = split(rows)
    products = dot(high, high) + dot(high, low) + dot(low, high)
    row = lax.broadcasted_iota(jnp.int32, (64, 128), 0)
    lane = lax.broadcasted_iota(jnp.int32, (64, 128), 1)
    energies = []
    for a in range(4):
        for k in range(4):
            b = a ^ k
            tile = complex_tile(products[128 * a : 128 * a + 128, 128 * b : 128 * b + 128])
            if k == 0:
                energies.append(jnp.sum(jnp.where(row == lane, tile, 0.0), axis=0, keepdims=True))
            at = 16 * a + 8 * (k % 2)
            for group in range(8):
                out_ref[2 * group + k // 2, at : at + 8, :] = tile[8 * group : 8 * group + 8]
    energies = jnp.concatenate(energies + [jnp.zeros((4, 128), jnp.float32)], axis=0)
    for place in range(16):
        out_ref[place, 64:, :] = energies


def sum_kernel(spread_ref, out_ref):
    total = spread_ref[0]
    for place in range(1, 16):
        total = total + spread_ref[place]
    for offset in range(4):
        to = member_index() ^ offset
        out_ref[to, :16, :] = total[16 * offset : 16 * offset + 16]
        for k in range(4):
            out_ref[to, 16 + k : 17 + k, :] = total[64 + (offset ^ k) : 65 + (offset ^ k)]
        out_ref[to, 20:, :] = jnp.zeros((4, 128), jnp.float32)


def far_kernel(own_ref, energy_ref, far_ref, out_ref):
    side = lax.axis_index("z1")
    passes = dot(own_ref[...], jnp.concatenate(split(far_ref[...].reshape(128, 2048)), axis=0))
    products = passes[:128, :128] + (passes[:128, 128:] + passes[128:, :128]) + passes[128:, 128:]
    here = complex_tile(products)
    there = complex_tile(products.T)
    for quarter in range(4):
        same = 4 * side + quarter
        other = 4 * (1 - side) + quarter
        out_ref[same, :16, :] = here[16 * quarter : 16 * quarter + 16]
        out_ref[other, :16, :] = there[16 * quarter : 16 * quarter + 16]
        out_ref[same, 16:, :] = jnp.zeros((8, 128), jnp.float32)
        out_ref[other, 16:, :] = energy_ref[...]


def pack_kernel(near_ref, far_ref, out_ref):
    far = far_ref[0]
    for place in range(1, 8):
        far = far + far_ref[place]
    near = near_ref[0, :16, :] + near_ref[1, :16, :] + near_ref[2, :16, :] + near_ref[3, :16, :]
    near = jnp.concatenate([modulus(near[:8]), modulus(near[8:])], axis=1)
    for place in range(16):
        out_ref[place, :16, :] = far[:16]
        out_ref[place, 16:24, :] = near
        out_ref[place, 24:, :] = far[16:]


def final_kernel(near_ref, shares_ref, out_ref):
    energies = near_ref[0, 16:, :64] + near_ref[1, 16:, :64] + near_ref[2, 16:, :64] + near_ref[3, 16:, :64]
    far_energies = shares_ref[0, 24:, :64]
    for place in range(1, 16):
        far_energies = far_energies + shares_ref[place, 24:, :64]
    inverse = 1.0 / jnp.sqrt(energies + EPSILON)
    far_inverse = 1.0 / jnp.sqrt(far_energies * 0.25 + EPSILON)
    columns = [inverse[k : k + 1] for k in range(4)] + [far_inverse[:1]]
    diagonal = lax.broadcasted_iota(jnp.int32, (64, 64), 0) == lax.broadcasted_iota(jnp.int32, (64, 64), 1)
    rows = jnp.sum(jnp.where(diagonal, columns[0], 0.0), axis=1, keepdims=True)
    for k in range(5):
        if k < 4:
            at = 64 * (k % 2)
            tile = [shares_ref[2 * group + k // 2, 16:24, at : at + 64] for group in range(8)]
            tile = jnp.concatenate(tile, axis=0)
        else:
            far = [sum(shares_ref[4 * y + quarter, :16, :] for y in range(4)) for quarter in range(4)]
            tile = modulus(jnp.concatenate(far, axis=0))
        out_ref[k] = tile * rows * columns[k]


def swapped(value, offset):
    pairs = [(source, source ^ offset) for source in range(4)]
    return lax.ppermute(value, QUAD, pairs)


def local(templates):
    templates = pltpu.with_memory_space_constraint(templates, pltpu.HBM)
    (quarter,) = quarters(templates, 3)
    three = swapped(quarter, 3)
    quarter, templates = lax.optimization_barrier((quarter, templates))
    first = half(templates, 0)
    passing = lax.ppermute(first, ("z1", "z0"), [(1, 2), (2, 1)])
    first, templates = lax.optimization_barrier((first, templates))
    mine, other, quarter = quarters(templates, 0, 1, 2)
    two = swapped(quarter, 2)
    one = swapped(other, 1)
    blocks = [mine, three, two, one]
    own, energy = call(own_kernel, (jax.ShapeDtypeStruct((256, 2048), jnp.bfloat16), f32(8, 128)), templates)
    second = half(templates, 2048)
    second, passing, own = lax.optimization_barrier((second, passing, own))
    onward = lax.ppermute(choose(second, passing), ("z1", "z0"), [(0, 2), (3, 1), (2, 3), (1, 0)])

    blocks, own = lax.optimization_barrier((blocks, own))
    spread = lax.all_to_all(call(near_kernel, f32(16, 72, 128), *blocks), BAND, 0, 0)
    near = lax.all_to_all(call(sum_kernel, f32(4, 24, 128), spread), QUAD, 0, 0)
    near, own = lax.optimization_barrier((near, own))
    far = lax.all_to_all(call(far_kernel, f32(8, 24, 128), own, energy, onward), FAR, 0, 0)
    shares = lax.all_to_all(call(pack_kernel, f32(16, 32, 128), near, far), BAND, 0, 0)
    return call(final_kernel, f32(5, 64, 64), near, shares).transpose(1, 0, 2)


def solution(mesh):
    devices = mesh.devices.reshape(4, 2, 2, 4, 2, 2, 2)
    finer = Mesh(devices, ("y", "x_lo", "core", "z_hi", "z1", "z0", "x_hi"))
    in_specs = (P(None, TMPL, BAND),)
    out_specs = P(TMPL, None, None)
    return jax.shard_map(local, mesh=finer, in_specs=in_specs, out_specs=out_specs, check_vma=False)
```

```python
import functools

import jax
import jax.numpy as jnp
from jax import lax
from jax.experimental import pallas as pl
from jax.experimental.pallas import tpu as pltpu
from jax.sharding import Mesh, PartitionSpec as P

BAND = ("y", "x_lo", "core")
QUAD = ("z0", "x_hi")
FAR = ("z1", "x_lo", "core")
TMPL = ("z_hi", "z1", "z0", "x_hi")
SCALE = 2.0**30
EPSILON = 1e-06 * 2.0**60
VMEM = pl.BlockSpec(memory_space=pltpu.VMEM)
HBM = pl.BlockSpec(memory_space=pltpu.HBM)


def call(kernel, shapes, *args, cost=None):
    return pl.pallas_call(
        kernel,
        cost_estimate=cost,
        out_shape=shapes,
        in_specs=[VMEM] * len(args),
        out_specs=jax.tree.map(lambda _: VMEM, shapes),
        compiler_params=pltpu.CompilerParams(vmem_limit_bytes=16 * 2**20),
    )(*args)


def f32(*shape):
    return jax.ShapeDtypeStruct(shape, jnp.float32)


def split(value):
    scaled = value * SCALE
    high = scaled.astype(jnp.bfloat16)
    low = (scaled - high.astype(jnp.float32)).astype(jnp.bfloat16)
    return high, low


def dot(left, right):
    return lax.dot_general(left, right, (((1,), (1,)), ((), ())), preferred_element_type=jnp.float32)


def four_passes(passes):
    return passes[:128, :128] + (passes[:128, 128:] + passes[128:, :128]) + passes[128:, 128:]


def complex_tile(products):
    lane = lax.broadcasted_iota(jnp.int32, (64, 128), 1)
    crossed = pltpu.roll(products[64:], 64, axis=1)
    return products[:64] + jnp.where(lane < 64, crossed, -crossed)


def modulus(tile):
    real_part = jnp.abs(tile[:, :64])
    imag_part = jnp.abs(tile[:, 64:])
    large = jnp.maximum(real_part, imag_part)
    small = jnp.minimum(real_part, imag_part)
    ratio = small / jnp.where(large > 0, large, 1.0)
    return large * jnp.sqrt(1.0 + ratio * ratio)


def member_index():
    return 2 * lax.axis_index("z0") + lax.axis_index("x_hi")


def is_middle():
    return lax.axis_index("z1") != lax.axis_index("z0")


def half_kernel(at, templates_ref, out_ref, sem):
    copy = pltpu.make_async_copy(templates_ref.at[:, :, at : at + 2048], out_ref, sem)
    copy.start()
    copy.wait()


def half(templates, at):
    return pl.pallas_call(
        functools.partial(half_kernel, at),
        out_shape=f32(2, 64, 2048),
        in_specs=[HBM],
        out_specs=VMEM,
        scratch_shapes=[pltpu.SemaphoreType.DMA],
        compiler_params=pltpu.CompilerParams(vmem_limit_bytes=8 * 2**20),
    )(templates)


def quarters_kernel(offsets, templates_ref, *refs):
    copies = []
    for place, offset in enumerate(offsets):
        at = pl.multiple_of((member_index() ^ offset) * 1024, 1024)
        copies.append(pltpu.make_async_copy(templates_ref.at[:, :, pl.ds(at, 1024)], refs[place], refs[-1].at[place]))
    for copy in copies:
        copy.start()
    for copy in copies:
        copy.wait()


def quarters(templates, *offsets):
    return pl.pallas_call(
        functools.partial(quarters_kernel, offsets),
        out_shape=(f32(2, 64, 1024),) * len(offsets),
        in_specs=[HBM],
        out_specs=(VMEM,) * len(offsets),
        scratch_shapes=[pltpu.SemaphoreType.DMA((len(offsets),))],
        compiler_params=pltpu.CompilerParams(vmem_limit_bytes=8 * 2**20),
    )(templates)


def choose_kernel(second_ref, passing_ref, out_ref, sem):
    @pl.when(is_middle())
    def _():
        copy = pltpu.make_async_copy(passing_ref, out_ref, sem)
        copy.start()
        copy.wait()

    @pl.when(jnp.logical_not(is_middle()))
    def _():
        copy = pltpu.make_async_copy(second_ref, out_ref, sem)
        copy.start()
        copy.wait()


def choose(second, passing):
    return pl.pallas_call(
        choose_kernel,
        out_shape=f32(2, 64, 2048),
        in_specs=[VMEM] * 2,
        out_specs=VMEM,
        scratch_shapes=[pltpu.SemaphoreType.DMA],
        compiler_params=pltpu.CompilerParams(vmem_limit_bytes=8 * 2**20),
    )(second, passing)


PAIRS = ((1, 0), (1, 2), (2, 0), (2, 1), (3, 0), (3, 1))


def pair_place(offset, k):
    high = 1 if k == 1 else 2
    return PAIRS.index((k, offset if offset & high == 0 else offset ^ k))


def is_second(k):
    return (member_index() & (1 if k == 1 else 2)) != 0


def own_kernel(templates_ref, own_ref, shares_ref):
    at = pl.multiple_of(jnp.where(is_middle(), 2048, 0), 2048)
    own_ref[...] = jnp.concatenate(split(templates_ref[:, :, pl.ds(at, 2048)].reshape(128, 2048)), axis=0)
    rows = jnp.concatenate(split(templates_ref[...].reshape(128, 4096)), axis=0)
    tile = complex_tile(four_passes(dot(rows, rows)))
    row = lax.broadcasted_iota(jnp.int32, (64, 128), 0)
    lane = lax.broadcasted_iota(jnp.int32, (64, 128), 1)
    energies = jnp.sum(jnp.where(row == lane, tile, 0.0), axis=0, keepdims=True)
    for place in range(16):
        shares_ref[place, :4, :] = tile[4 * place : 4 * place + 4]
        shares_ref[place, 4:5, :] = energies
        shares_ref[place, 5:, :] = jnp.zeros((3, 128), jnp.float32)


def near_kernel(itself_ref, own_ref, three_ref, two_ref, one_ref, out_ref):
    blocks = [own_ref[...], one_ref[...], two_ref[...], three_ref[...]]
    rows = jnp.concatenate([block.reshape(128, 1024) for block in blocks], axis=0)
    high, low = split(rows)
    products = dot(high, high) + dot(high, low) + dot(low, high)

    def tile_of(a, b):
        return complex_tile(products[128 * a : 128 * a + 128, 128 * b : 128 * b + 128])

    for place, (k, offset) in enumerate(PAIRS):
        tile = jnp.where(is_second(k), tile_of(offset ^ k, offset), tile_of(offset, offset ^ k))
        for to in range(16):
            out_ref[to, 4 * place : 4 * place + 4, :] = tile[4 * to : 4 * to + 4]
    out_ref[:, 24:, :] = itself_ref[...]


def total_of(ref):
    total = ref[0]
    for place in range(1, ref.shape[0]):
        total = total + ref[place]
    return total


def sum_kernel(spread_ref, out_ref, itself_ref):
    total = total_of(spread_ref)
    itself_ref[...] = total[24:]
    energies = total[28:29]
    for offset in range(4):
        to = member_index() ^ offset
        for k in range(1, 4):
            at = 4 * pair_place(offset, k)
            out_ref[to, 4 * k - 4 : 4 * k, :] = total[at : at + 4]
        out_ref[to, 12:13, :] = energies
        out_ref[to, 13:, :] = jnp.zeros((3, 128), jnp.float32)


def far_kernel(near_ref, own_ref, far_ref, out_ref):
    side = lax.axis_index("z1")
    far = jnp.concatenate(split(far_ref[...].reshape(128, 2048)), axis=0)
    products = four_passes(dot(own_ref[...], far))
    here = complex_tile(products)
    there = complex_tile(products.T)
    energies = near_ref[member_index(), 12:13, :]
    for quarter in range(4):
        same = 4 * side + quarter
        other = 4 * (1 - side) + quarter
        out_ref[same, :16, :] = here[16 * quarter : 16 * quarter + 16]
        out_ref[other, :16, :] = there[16 * quarter : 16 * quarter + 16]
        out_ref[same, 16:, :] = jnp.zeros((8, 128), jnp.float32)
        out_ref[other, 16:17, :] = energies
        out_ref[other, 17:, :] = jnp.zeros((7, 128), jnp.float32)


def pack_kernel(near_ref, itself_ref, far_ref, out_ref):
    far = total_of(far_ref)[:16]
    near = total_of(near_ref)
    tiles = [itself_ref[:4, :]] + [near[4 * k - 4 : 4 * k] for k in range(1, 4)]
    tiles = [modulus(tile) for tile in tiles]
    first = jnp.concatenate(tiles[:2], axis=1)
    second = jnp.concatenate(tiles[2:], axis=1)
    for place in range(16):
        out_ref[place, :16, :] = far
        out_ref[place, 16:20, :] = first
        out_ref[place, 20:, :] = second


def final_kernel(near_ref, far_ref, shares_ref, out_ref):
    energies = [near_ref[member_index() ^ k, 12:13, :64] for k in range(4)]
    energies.append(total_of(far_ref)[16:17, :64] * 0.25)
    columns = [1.0 / jnp.sqrt(energy + EPSILON) for energy in energies]
    diagonal = lax.broadcasted_iota(jnp.int32, (64, 64), 0) == lax.broadcasted_iota(jnp.int32, (64, 64), 1)
    rows = jnp.sum(jnp.where(diagonal, columns[0], 0.0), axis=1, keepdims=True)
    for k in range(5):
        if k < 4:
            at, lane = 16 + 4 * (k // 2), 64 * (k % 2)
            tile = [shares_ref[place, at : at + 4, lane : lane + 64] for place in range(16)]
            tile = jnp.concatenate(tile, axis=0)
            if k > 0:
                tile = jnp.where(is_second(k), tile.T, tile)
        else:
            far = [sum(shares_ref[4 * y + quarter, :16, :] for y in range(4)) for quarter in range(4)]
            tile = modulus(jnp.concatenate(far, axis=0))
        out_ref[k] = tile * rows * columns[k]


def swapped(value, offset):
    pairs = [(source, source ^ offset) for source in range(4)]
    return lax.ppermute(value, QUAD, pairs)


def local(templates):
    templates = pltpu.with_memory_space_constraint(templates, pltpu.HBM)
    (quarter,) = quarters(templates, 3)
    three = swapped(quarter, 3)
    quarter, templates = lax.optimization_barrier((quarter, templates))
    first = half(templates, 0)
    passing = lax.ppermute(first, ("z1", "z0"), [(1, 2), (2, 1)])
    first, templates = lax.optimization_barrier((first, templates))
    mine, other, quarter = quarters(templates, 0, 1, 2)
    two = swapped(quarter, 2)
    one = swapped(other, 1)
    blocks = [mine, three, two, one]
    second = half(templates, 2048)
    second, templates = lax.optimization_barrier((second, templates))
    own, shares = call(own_kernel, (jax.ShapeDtypeStruct((256, 2048), jnp.bfloat16), f32(16, 8, 128)), templates)
    second, passing, own = lax.optimization_barrier((second, passing, own))
    onward = lax.ppermute(choose(second, passing), ("z1", "z0"), [(0, 2), (3, 1), (2, 3), (1, 0)])

    blocks, own = lax.optimization_barrier((blocks, own))
    cost = pl.CostEstimate(flops=46 * 10**9, bytes_accessed=4 * 2**20, transcendentals=0)
    spread = lax.all_to_all(call(near_kernel, f32(16, 32, 128), shares, *blocks, cost=cost), BAND, 0, 0)
    to_quad, itself = call(sum_kernel, (f32(4, 16, 128), f32(8, 128)), spread)
    near = lax.all_to_all(to_quad, QUAD, 0, 0)
    near, own = lax.optimization_barrier((near, own))
    far = lax.all_to_all(call(far_kernel, f32(8, 24, 128), near, own, onward), FAR, 0, 0)
    shares = lax.all_to_all(call(pack_kernel, f32(16, 24, 128), near, itself, far), BAND, 0, 0)
    return call(final_kernel, f32(5, 64, 64), near, far, shares).transpose(1, 0, 2)


def solution(mesh):
    devices = mesh.devices.reshape(4, 2, 2, 4, 2, 2, 2)
    finer = Mesh(devices, ("y", "x_lo", "core", "z_hi", "z1", "z0", "x_hi"))
    in_specs = (P(None, TMPL, BAND),)
    out_specs = P(TMPL, None, None)
    return jax.shard_map(local, mesh=finer, in_specs=in_specs, out_specs=out_specs, check_vma=False)
```

```python
import functools

import jax
import jax.numpy as jnp
from jax import lax
from jax.experimental import pallas as pl
from jax.experimental.pallas import tpu as pltpu
from jax.sharding import Mesh, PartitionSpec as P

BAND = ("y", "x_lo", "core")
QUAD = ("z0", "x_hi")
FAR = ("z1", "x_lo", "core")
TMPL = ("z_hi", "z1", "z0", "x_hi")
SCALE = 2.0**30
EPSILON = 1e-06 * 2.0**60
VMEM = pl.BlockSpec(memory_space=pltpu.VMEM)
HBM = pl.BlockSpec(memory_space=pltpu.HBM)


def call(kernel, shapes, *args, cost=None, scratch=()):
    return pl.pallas_call(
        kernel,
        scratch_shapes=scratch,
        cost_estimate=cost,
        out_shape=shapes,
        in_specs=[VMEM] * len(args),
        out_specs=jax.tree.map(lambda _: VMEM, shapes),
        compiler_params=pltpu.CompilerParams(vmem_limit_bytes=16 * 2**20),
    )(*args)


def f32(*shape):
    return jax.ShapeDtypeStruct(shape, jnp.float32)


def split(value):
    scaled = value * SCALE
    high = scaled.astype(jnp.bfloat16)
    low = (scaled - high.astype(jnp.float32)).astype(jnp.bfloat16)
    return high, low


def dot(left, right):
    return lax.dot_general(left, right, (((1,), (1,)), ((), ())), preferred_element_type=jnp.float32)


def four_passes(passes):
    return passes[:128, :128] + (passes[:128, 128:] + passes[128:, :128]) + passes[128:, 128:]


def complex_tile(products):
    lane = lax.broadcasted_iota(jnp.int32, (64, 128), 1)
    crossed = pltpu.roll(products[64:], 64, axis=1)
    return products[:64] + jnp.where(lane < 64, crossed, -crossed)


def modulus(tile):
    real_part = jnp.abs(tile[:, :64])
    imag_part = jnp.abs(tile[:, 64:])
    large = jnp.maximum(real_part, imag_part)
    small = jnp.minimum(real_part, imag_part)
    ratio = small / jnp.where(large > 0, large, 1.0)
    return large * jnp.sqrt(1.0 + ratio * ratio)


def member_index():
    return 2 * lax.axis_index("z0") + lax.axis_index("x_hi")


def is_middle():
    return lax.axis_index("z1") != lax.axis_index("z0")


def cut_kernel(pieces, templates_ref, *refs):
    copies = []
    for place, (kind, which) in enumerate(pieces):
        if kind == "half":
            source = templates_ref.at[:, :, 2048 * which : 2048 * which + 2048]
        else:
            at = pl.multiple_of((member_index() ^ which) * 1024, 1024)
            source = templates_ref.at[:, :, pl.ds(at, 1024)]
        copies.append(pltpu.make_async_copy(source, refs[place], refs[-1].at[place]))
    for copy in copies:
        copy.start()
    for copy in copies:
        copy.wait()


def cut(templates, *pieces):
    return pl.pallas_call(
        functools.partial(cut_kernel, pieces),
        out_shape=tuple(f32(2, 64, 2048 if kind == "half" else 1024) for kind, _ in pieces),
        in_specs=[HBM],
        out_specs=(VMEM,) * len(pieces),
        scratch_shapes=[pltpu.SemaphoreType.DMA((len(pieces),))],
        compiler_params=pltpu.CompilerParams(vmem_limit_bytes=8 * 2**20),
    )(templates)


def choose_kernel(second_ref, passing_ref, out_ref, sem):
    @pl.when(is_middle())
    def _():
        copy = pltpu.make_async_copy(passing_ref, out_ref, sem)
        copy.start()
        copy.wait()

    @pl.when(jnp.logical_not(is_middle()))
    def _():
        copy = pltpu.make_async_copy(second_ref, out_ref, sem)
        copy.start()
        copy.wait()


def choose(second, passing):
    return pl.pallas_call(
        choose_kernel,
        out_shape=f32(2, 64, 2048),
        in_specs=[VMEM] * 2,
        out_specs=VMEM,
        scratch_shapes=[pltpu.SemaphoreType.DMA],
        compiler_params=pltpu.CompilerParams(vmem_limit_bytes=8 * 2**20),
    )(second, passing)


PAIRS = ((0, 1), (0, 2), (0, 3), (1, 2), (1, 3), (2, 3))


def is_second(k):
    return (member_index() & (1 if k == 1 else 2)) != 0


def own_kernel(templates_ref, own_ref, shares_ref):
    at = pl.multiple_of(jnp.where(is_middle(), 2048, 0), 2048)
    own_ref[...] = jnp.concatenate(split(templates_ref[:, :, pl.ds(at, 2048)].reshape(128, 2048)), axis=0)
    rows = jnp.concatenate(split(templates_ref[...].reshape(128, 4096)), axis=0)
    tile = complex_tile(four_passes(dot(rows, rows)))
    row = lax.broadcasted_iota(jnp.int32, (64, 128), 0)
    lane = lax.broadcasted_iota(jnp.int32, (64, 128), 1)
    energies = jnp.sum(jnp.where(row == lane, tile, 0.0), axis=0, keepdims=True)
    for place in range(16):
        shares_ref[place, :4, :] = tile[4 * place : 4 * place + 4]
        shares_ref[place, 4:5, :] = energies
        shares_ref[place, 5:, :] = jnp.zeros((3, 128), jnp.float32)


def near_kernel(itself_ref, own_ref, three_ref, one_ref, two_ref, out_ref, high_ref, low_ref):
    for offset, ref in enumerate((own_ref, one_ref, two_ref, three_ref)):
        high, low = split(ref[...].reshape(128, 1024))
        high_ref[member_index() ^ offset] = high
        low_ref[member_index() ^ offset] = low
    for a in range(3):
        right_high = high_ref[a + 1 :].reshape(128 * (3 - a), 1024)
        right_low = low_ref[a + 1 :].reshape(128 * (3 - a), 1024)
        left = jnp.concatenate([high_ref[a], low_ref[a]], axis=0)
        passes = dot(left, right_high)
        products = passes[:128] + passes[128:] + dot(high_ref[a], right_low)
        for b in range(a + 1, 4):
            at = 128 * (b - a - 1)
            tile = complex_tile(products[:, at : at + 128])
            place = 4 * PAIRS.index((a, b))
            for to in range(16):
                out_ref[to, place : place + 4, :] = tile[4 * to : 4 * to + 4]
    out_ref[:, 24:, :] = itself_ref[...]


def total_of(ref):
    total = ref[0]
    for place in range(1, ref.shape[0]):
        total = total + ref[place]
    return total


def sum_kernel(spread_ref, out_ref, itself_ref):
    total = total_of(spread_ref)
    itself_ref[...] = total[24:]
    energies = total[28:29]
    for to in range(4):
        for k in range(1, 4):
            at = 4 * PAIRS.index((min(to, to ^ k), max(to, to ^ k)))
            out_ref[to, 4 * k - 4 : 4 * k, :] = total[at : at + 4]
        out_ref[to, 12:13, :] = energies
        out_ref[to, 13:, :] = jnp.zeros((3, 128), jnp.float32)


def far_kernel(near_ref, own_ref, far_ref, out_ref):
    side = lax.axis_index("z1")
    far = jnp.concatenate(split(far_ref[...].reshape(128, 2048)), axis=0)
    products = four_passes(dot(own_ref[...], far))
    here = complex_tile(products)
    there = complex_tile(products.T)
    energies = near_ref[member_index(), 12:13, :]
    for quarter in range(4):
        same = 4 * side + quarter
        other = 4 * (1 - side) + quarter
        out_ref[same, :16, :] = here[16 * quarter : 16 * quarter + 16]
        out_ref[other, :16, :] = there[16 * quarter : 16 * quarter + 16]
        out_ref[same, 16:, :] = jnp.zeros((8, 128), jnp.float32)
        out_ref[other, 16:17, :] = energies
        out_ref[other, 17:, :] = jnp.zeros((7, 128), jnp.float32)


def pack_kernel(near_ref, itself_ref, far_ref, out_ref):
    far = total_of(far_ref)[:16]
    near = total_of(near_ref)
    tiles = [itself_ref[:4, :]] + [near[4 * k - 4 : 4 * k] for k in range(1, 4)]
    tiles = [modulus(tile) for tile in tiles]
    first = jnp.concatenate(tiles[:2], axis=1)
    second = jnp.concatenate(tiles[2:], axis=1)
    for place in range(16):
        out_ref[place, :16, :] = far
        out_ref[place, 16:20, :] = first
        out_ref[place, 20:, :] = second


def final_kernel(near_ref, far_ref, shares_ref, out_ref):
    energies = [near_ref[member_index() ^ k, 12:13, :64] for k in range(4)]
    energies.append(total_of(far_ref)[16:17, :64] * 0.25)
    columns = [1.0 / jnp.sqrt(energy + EPSILON) for energy in energies]
    diagonal = lax.broadcasted_iota(jnp.int32, (64, 64), 0) == lax.broadcasted_iota(jnp.int32, (64, 64), 1)
    rows = jnp.sum(jnp.where(diagonal, columns[0], 0.0), axis=1, keepdims=True)
    for k in range(5):
        if k < 4:
            at, lane = 16 + 4 * (k // 2), 64 * (k % 2)
            tile = [shares_ref[place, at : at + 4, lane : lane + 64] for place in range(16)]
            tile = jnp.concatenate(tile, axis=0)
            if k > 0:
                tile = jnp.where(is_second(k), tile.T, tile)
        else:
            far = [sum(shares_ref[4 * y + quarter, :16, :] for y in range(4)) for quarter in range(4)]
            tile = modulus(jnp.concatenate(far, axis=0))
        out_ref[k] = tile * rows * columns[k]


def swapped(value, offset):
    pairs = [(source, source ^ offset) for source in range(4)]
    return lax.ppermute(value, QUAD, pairs)


def local(templates):
    templates = pltpu.with_memory_space_constraint(templates, pltpu.HBM)
    first, third = cut(templates, ("half", 0), ("quarter", 3))
    passing = lax.ppermute(first, ("z1", "z0"), [(1, 2), (2, 1)])
    three = swapped(third, 3)
    third, templates = lax.optimization_barrier((third, templates))
    other, nearest, mine = cut(templates, ("quarter", 2), ("quarter", 1), ("quarter", 0))
    blocks = [mine, three, swapped(nearest, 1), swapped(other, 2)]
    other, templates = lax.optimization_barrier((other, templates))
    (second,) = cut(templates, ("half", 1))
    second, templates = lax.optimization_barrier((second, templates))
    own, shares = call(own_kernel, (jax.ShapeDtypeStruct((256, 2048), jnp.bfloat16), f32(16, 8, 128)), templates)
    second, passing, own = lax.optimization_barrier((second, passing, own))
    outgoing = choose(second, passing)
    onward = lax.ppermute(outgoing, ("z1", "z0"), [(0, 2), (3, 1), (2, 3), (1, 0)])

    blocks, own, outgoing = lax.optimization_barrier((blocks, own, outgoing))
    cost = pl.CostEstimate(flops=46 * 10**9, bytes_accessed=4 * 2**20, transcendentals=0)
    terms = (pltpu.VMEM((4, 128, 1024), jnp.bfloat16),) * 2
    spread = call(near_kernel, f32(16, 32, 128), shares, *blocks, cost=cost, scratch=terms)
    spread = lax.all_to_all(spread, BAND, 0, 0)
    to_quad, itself = call(sum_kernel, (f32(4, 16, 128), f32(8, 128)), spread)
    near = lax.all_to_all(to_quad, QUAD, 0, 0)
    near, own = lax.optimization_barrier((near, own))
    far = lax.all_to_all(call(far_kernel, f32(8, 24, 128), near, own, onward), FAR, 0, 0)
    shares = lax.all_to_all(call(pack_kernel, f32(16, 24, 128), near, itself, far), BAND, 0, 0)
    return call(final_kernel, f32(5, 64, 64), near, far, shares).transpose(1, 0, 2)


def solution(mesh):
    devices = mesh.devices.reshape(4, 2, 2, 4, 2, 2, 2)
    finer = Mesh(devices, ("y", "x_lo", "core", "z_hi", "z1", "z0", "x_hi"))
    in_specs = (P(None, TMPL, BAND),)
    out_specs = P(TMPL, None, None)
    return jax.shard_map(local, mesh=finer, in_specs=in_specs, out_specs=out_specs, check_vma=False)
```

```python
import functools

import jax
import jax.numpy as jnp
from jax import lax
from jax.experimental import pallas as pl
from jax.experimental.pallas import tpu as pltpu
from jax.sharding import Mesh, PartitionSpec as P

BAND = ("y", "x_lo", "core")
QUAD = ("z0", "x_hi")
FAR = ("z1", "x_lo", "core")
TMPL = ("z_hi", "z1", "z0", "x_hi")
SCALE = 2.0**30
EPSILON = 1e-06 * 2.0**60
VMEM = pl.BlockSpec(memory_space=pltpu.VMEM)
HBM = pl.BlockSpec(memory_space=pltpu.HBM)


def call(kernel, shapes, *args, cost=None, scratch=()):
    return pl.pallas_call(
        kernel,
        scratch_shapes=scratch,
        cost_estimate=cost,
        out_shape=shapes,
        in_specs=[VMEM] * len(args),
        out_specs=jax.tree.map(lambda _: VMEM, shapes),
        compiler_params=pltpu.CompilerParams(vmem_limit_bytes=16 * 2**20),
    )(*args)


def f32(*shape):
    return jax.ShapeDtypeStruct(shape, jnp.float32)


def split(value):
    scaled = value * SCALE
    high = scaled.astype(jnp.bfloat16)
    low = (scaled - high.astype(jnp.float32)).astype(jnp.bfloat16)
    return high, low


def dot(left, right):
    return lax.dot_general(left, right, (((1,), (1,)), ((), ())), preferred_element_type=jnp.float32)


def four_passes(passes):
    return passes[:128, :128] + (passes[:128, 128:] + passes[128:, :128]) + passes[128:, 128:]


def complex_tile(products):
    lane = lax.broadcasted_iota(jnp.int32, (64, 128), 1)
    crossed = pltpu.roll(products[64:], 64, axis=1)
    return products[:64] + jnp.where(lane < 64, crossed, -crossed)


def modulus(tile):
    real_part = jnp.abs(tile[:, :64])
    imag_part = jnp.abs(tile[:, 64:])
    large = jnp.maximum(real_part, imag_part)
    small = jnp.minimum(real_part, imag_part)
    ratio = small / jnp.where(large > 0, large, 1.0)
    return large * jnp.sqrt(1.0 + ratio * ratio)


def member_index():
    return 2 * lax.axis_index("z0") + lax.axis_index("x_hi")


def is_middle():
    return lax.axis_index("z1") != lax.axis_index("z0")


def cut_kernel(pieces, templates_ref, *refs):
    copies = []
    for place, (kind, which) in enumerate(pieces):
        if kind == "half":
            source = templates_ref.at[:, :, 2048 * which : 2048 * which + 2048]
        else:
            at = pl.multiple_of((member_index() ^ which) * 1024, 1024)
            source = templates_ref.at[:, :, pl.ds(at, 1024)]
        copies.append(pltpu.make_async_copy(source, refs[place], refs[-1].at[place]))
    for copy in copies:
        copy.start()
    for copy in copies:
        copy.wait()


def cut(templates, *pieces):
    return pl.pallas_call(
        functools.partial(cut_kernel, pieces),
        out_shape=tuple(f32(2, 64, 2048 if kind == "half" else 1024) for kind, _ in pieces),
        in_specs=[HBM],
        out_specs=(VMEM,) * len(pieces),
        scratch_shapes=[pltpu.SemaphoreType.DMA((len(pieces),))],
        compiler_params=pltpu.CompilerParams(vmem_limit_bytes=8 * 2**20),
    )(templates)


def choose_kernel(second_ref, passing_ref, out_ref, sem):
    @pl.when(is_middle())
    def _():
        copy = pltpu.make_async_copy(passing_ref, out_ref, sem)
        copy.start()
        copy.wait()

    @pl.when(jnp.logical_not(is_middle()))
    def _():
        copy = pltpu.make_async_copy(second_ref, out_ref, sem)
        copy.start()
        copy.wait()


def choose(second, passing):
    return pl.pallas_call(
        choose_kernel,
        out_shape=f32(2, 64, 2048),
        in_specs=[VMEM] * 2,
        out_specs=VMEM,
        scratch_shapes=[pltpu.SemaphoreType.DMA],
        compiler_params=pltpu.CompilerParams(vmem_limit_bytes=8 * 2**20),
    )(second, passing)


PAIRS = ((0, 1), (0, 2), (0, 3), (1, 2), (1, 3), (2, 3))


def is_second(k):
    return (member_index() & (1 if k == 1 else 2)) != 0


def own_kernel(templates_ref, own_ref, shares_ref):
    at = pl.multiple_of(jnp.where(is_middle(), 2048, 0), 2048)
    own_ref[...] = jnp.concatenate(split(templates_ref[:, :, pl.ds(at, 2048)].reshape(128, 2048)), axis=0)
    rows = jnp.concatenate(split(templates_ref[...].reshape(128, 4096)), axis=0)
    tile = complex_tile(four_passes(dot(rows, rows)))
    row = lax.broadcasted_iota(jnp.int32, (64, 128), 0)
    lane = lax.broadcasted_iota(jnp.int32, (64, 128), 1)
    energies = jnp.sum(jnp.where(row == lane, tile, 0.0), axis=0, keepdims=True)
    for place in range(16):
        shares_ref[place, :4, :] = tile[4 * place : 4 * place + 4]
        shares_ref[place, 4:5, :] = energies
        shares_ref[place, 5:, :] = jnp.zeros((3, 128), jnp.float32)


def near_kernel(itself_ref, own_ref, three_ref, one_ref, two_ref, out_ref, high_ref, low_ref):
    for offset, ref in enumerate((own_ref, one_ref, two_ref, three_ref)):
        high, low = split(ref[...].reshape(128, 1024))
        high_ref[member_index() ^ offset] = high
        low_ref[member_index() ^ offset] = low

    def both(a):
        return jnp.concatenate([high_ref[a], low_ref[a]], axis=0)

    left = jnp.concatenate([high_ref[0], high_ref[1], low_ref[0], low_ref[1]], axis=0)
    passes = dot(left, jnp.concatenate([high_ref[2], high_ref[3]], axis=0))
    across = dot(left[:256], jnp.concatenate([low_ref[2], low_ref[3]], axis=0)) + passes[256:] + passes[:256]
    products = {(0, 1): four_passes(dot(both(0), both(1))), (2, 3): four_passes(dot(both(2), both(3)))}
    for a in range(2):
        for b in range(2):
            products[a, b + 2] = across[128 * a : 128 * a + 128, 128 * b : 128 * b + 128]
    for place, pair in enumerate(PAIRS):
        tile = complex_tile(products[pair])
        for to in range(16):
            out_ref[to, 4 * place : 4 * place + 4, :] = tile[4 * to : 4 * to + 4]
    out_ref[:, 24:, :] = itself_ref[...]


def total_of(ref):
    total = ref[0]
    for place in range(1, ref.shape[0]):
        total = total + ref[place]
    return total


def sum_kernel(spread_ref, out_ref, itself_ref):
    total = total_of(spread_ref)
    itself_ref[...] = total[24:]
    energies = total[28:29]
    for to in range(4):
        for k in range(1, 4):
            at = 4 * PAIRS.index((min(to, to ^ k), max(to, to ^ k)))
            out_ref[to, 4 * k - 4 : 4 * k, :] = total[at : at + 4]
        out_ref[to, 12:13, :] = energies
        out_ref[to, 13:, :] = jnp.zeros((3, 128), jnp.float32)


def far_kernel(near_ref, own_ref, far_ref, out_ref):
    side = lax.axis_index("z1")
    far = jnp.concatenate(split(far_ref[...].reshape(128, 2048)), axis=0)
    products = four_passes(dot(own_ref[...], far))
    here = complex_tile(products)
    there = complex_tile(products.T)
    energies = near_ref[member_index(), 12:13, :]
    for quarter in range(4):
        same = 4 * side + quarter
        other = 4 * (1 - side) + quarter
        out_ref[same, :16, :] = here[16 * quarter : 16 * quarter + 16]
        out_ref[other, :16, :] = there[16 * quarter : 16 * quarter + 16]
        out_ref[same, 16:, :] = jnp.zeros((8, 128), jnp.float32)
        out_ref[other, 16:17, :] = energies
        out_ref[other, 17:, :] = jnp.zeros((7, 128), jnp.float32)


def pack_kernel(near_ref, itself_ref, far_ref, out_ref):
    far = total_of(far_ref)[:16]
    near = total_of(near_ref)
    tiles = [itself_ref[:4, :]] + [near[4 * k - 4 : 4 * k] for k in range(1, 4)]
    tiles = [modulus(tile) for tile in tiles]
    first = jnp.concatenate(tiles[:2], axis=1)
    second = jnp.concatenate(tiles[2:], axis=1)
    for place in range(16):
        out_ref[place, :16, :] = far
        out_ref[place, 16:20, :] = first
        out_ref[place, 20:, :] = second


def final_kernel(near_ref, far_ref, shares_ref, out_ref):
    energies = [near_ref[member_index() ^ k, 12:13, :64] for k in range(4)]
    energies.append(total_of(far_ref)[16:17, :64] * 0.25)
    columns = [1.0 / jnp.sqrt(energy + EPSILON) for energy in energies]
    diagonal = lax.broadcasted_iota(jnp.int32, (64, 64), 0) == lax.broadcasted_iota(jnp.int32, (64, 64), 1)
    rows = jnp.sum(jnp.where(diagonal, columns[0], 0.0), axis=1, keepdims=True)
    for k in range(5):
        if k < 4:
            at, lane = 16 + 4 * (k // 2), 64 * (k % 2)
            tile = [shares_ref[place, at : at + 4, lane : lane + 64] for place in range(16)]
            tile = jnp.concatenate(tile, axis=0)
            if k > 0:
                tile = jnp.where(is_second(k), tile.T, tile)
        else:
            far = [sum(shares_ref[4 * y + quarter, :16, :] for y in range(4)) for quarter in range(4)]
            tile = modulus(jnp.concatenate(far, axis=0))
        out_ref[k] = tile * rows * columns[k]


def swapped(value, offset):
    pairs = [(source, source ^ offset) for source in range(4)]
    return lax.ppermute(value, QUAD, pairs)


def local(templates):
    templates = pltpu.with_memory_space_constraint(templates, pltpu.HBM)
    first, third = cut(templates, ("half", 0), ("quarter", 3))
    passing = lax.ppermute(first, ("z1", "z0"), [(1, 2), (2, 1)])
    three = swapped(third, 3)
    third, templates = lax.optimization_barrier((third, templates))
    other, nearest, mine = cut(templates, ("quarter", 2), ("quarter", 1), ("quarter", 0))
    blocks = [mine, three, swapped(nearest, 1), swapped(other, 2)]
    other, templates = lax.optimization_barrier((other, templates))
    (second,) = cut(templates, ("half", 1))
    second, templates = lax.optimization_barrier((second, templates))
    own, shares = call(own_kernel, (jax.ShapeDtypeStruct((256, 2048), jnp.bfloat16), f32(16, 8, 128)), templates)
    second, passing, own = lax.optimization_barrier((second, passing, own))
    outgoing = choose(second, passing)
    onward = lax.ppermute(outgoing, ("z1", "z0"), [(0, 2), (3, 1), (2, 3), (1, 0)])

    blocks, own, outgoing = lax.optimization_barrier((blocks, own, outgoing))
    cost = pl.CostEstimate(flops=46 * 10**9, bytes_accessed=4 * 2**20, transcendentals=0)
    terms = (pltpu.VMEM((4, 128, 1024), jnp.bfloat16),) * 2
    spread = call(near_kernel, f32(16, 32, 128), shares, *blocks, cost=cost, scratch=terms)
    spread = lax.all_to_all(spread, BAND, 0, 0)
    to_quad, itself = call(sum_kernel, (f32(4, 16, 128), f32(8, 128)), spread)
    near = lax.all_to_all(to_quad, QUAD, 0, 0)
    near, own = lax.optimization_barrier((near, own))
    far = lax.all_to_all(call(far_kernel, f32(8, 24, 128), near, own, onward), FAR, 0, 0)
    shares = lax.all_to_all(call(pack_kernel, f32(16, 24, 128), near, itself, far), BAND, 0, 0)
    return call(final_kernel, f32(5, 64, 64), near, far, shares).transpose(1, 0, 2)


def solution(mesh):
    devices = mesh.devices.reshape(4, 2, 2, 4, 2, 2, 2)
    finer = Mesh(devices, ("y", "x_lo", "core", "z_hi", "z1", "z0", "x_hi"))
    in_specs = (P(None, TMPL, BAND),)
    out_specs = P(TMPL, None, None)
    return jax.shard_map(local, mesh=finer, in_specs=in_specs, out_specs=out_specs, check_vma=False)
```

```python
import functools

import jax
import jax.numpy as jnp
from jax import lax
from jax.experimental import pallas as pl
from jax.experimental.pallas import tpu as pltpu
from jax.sharding import Mesh, PartitionSpec as P

BAND = ("y", "x_lo", "core")
QUAD = ("z0", "x_hi")
FAR = ("z1", "x_lo", "core")
TMPL = ("z_hi", "z1", "z0", "x_hi")
SCALE = 2.0**30
EPSILON = 1e-06 * 2.0**60
VMEM = pl.BlockSpec(memory_space=pltpu.VMEM)
HBM = pl.BlockSpec(memory_space=pltpu.HBM)


def call(kernel, shapes, *args, cost=None, scratch=()):
    return pl.pallas_call(
        kernel,
        scratch_shapes=scratch,
        cost_estimate=cost,
        out_shape=shapes,
        in_specs=[VMEM] * len(args),
        out_specs=jax.tree.map(lambda _: VMEM, shapes),
        compiler_params=pltpu.CompilerParams(vmem_limit_bytes=16 * 2**20),
    )(*args)


def f32(*shape):
    return jax.ShapeDtypeStruct(shape, jnp.float32)


def split(value):
    scaled = value * SCALE
    high = scaled.astype(jnp.bfloat16)
    low = (scaled - high.astype(jnp.float32)).astype(jnp.bfloat16)
    return high, low


def dot(left, right):
    return lax.dot_general(left, right, (((1,), (1,)), ((), ())), preferred_element_type=jnp.float32)


def four_passes(passes):
    return passes[:128, :128] + (passes[:128, 128:] + passes[128:, :128]) + passes[128:, 128:]


def complex_tile(products):
    lane = lax.broadcasted_iota(jnp.int32, (64, 128), 1)
    crossed = pltpu.roll(products[64:], 64, axis=1)
    return products[:64] + jnp.where(lane < 64, crossed, -crossed)


def modulus(tile):
    real_part = jnp.abs(tile[:, :64])
    imag_part = jnp.abs(tile[:, 64:])
    large = jnp.maximum(real_part, imag_part)
    small = jnp.minimum(real_part, imag_part)
    ratio = small / jnp.where(large > 0, large, 1.0)
    return large * jnp.sqrt(1.0 + ratio * ratio)


def member_index():
    return 2 * lax.axis_index("z0") + lax.axis_index("x_hi")


def is_middle():
    return lax.axis_index("z1") != lax.axis_index("z0")


def cut_kernel(pieces, templates_ref, *refs):
    copies = []
    for place, (kind, which) in enumerate(pieces):
        if kind == "half":
            source = templates_ref.at[:, :, 2048 * which : 2048 * which + 2048]
        else:
            at = pl.multiple_of((member_index() ^ which) * 1024, 1024)
            source = templates_ref.at[:, :, pl.ds(at, 1024)]
        copies.append(pltpu.make_async_copy(source, refs[place], refs[-1].at[place]))
    for copy in copies:
        copy.start()
    for copy in copies:
        copy.wait()


def cut(templates, *pieces):
    return pl.pallas_call(
        functools.partial(cut_kernel, pieces),
        out_shape=tuple(f32(2, 64, 2048 if kind == "half" else 1024) for kind, _ in pieces),
        in_specs=[HBM],
        out_specs=(VMEM,) * len(pieces),
        scratch_shapes=[pltpu.SemaphoreType.DMA((len(pieces),))],
        compiler_params=pltpu.CompilerParams(vmem_limit_bytes=8 * 2**20),
    )(templates)


def choose_kernel(second_ref, passing_ref, out_ref, sem):
    @pl.when(is_middle())
    def _():
        copy = pltpu.make_async_copy(passing_ref, out_ref, sem)
        copy.start()
        copy.wait()

    @pl.when(jnp.logical_not(is_middle()))
    def _():
        copy = pltpu.make_async_copy(second_ref, out_ref, sem)
        copy.start()
        copy.wait()


def choose(second, passing):
    return pl.pallas_call(
        choose_kernel,
        out_shape=f32(2, 64, 2048),
        in_specs=[VMEM] * 2,
        out_specs=VMEM,
        scratch_shapes=[pltpu.SemaphoreType.DMA],
        compiler_params=pltpu.CompilerParams(vmem_limit_bytes=8 * 2**20),
    )(second, passing)


PAIRS = ((0, 1), (0, 2), (0, 3), (1, 2), (1, 3), (2, 3))


def is_second(k):
    return (member_index() & (1 if k == 1 else 2)) != 0


def own_kernel(templates_ref, own_ref, shares_ref):
    at = pl.multiple_of(jnp.where(is_middle(), 2048, 0), 2048)
    own_ref[...] = jnp.concatenate(split(templates_ref[:, :, pl.ds(at, 2048)].reshape(128, 2048)), axis=0)
    rows = jnp.concatenate(split(templates_ref[...].reshape(128, 4096)), axis=0)
    tile = complex_tile(four_passes(dot(rows, rows)))
    row = lax.broadcasted_iota(jnp.int32, (64, 128), 0)
    lane = lax.broadcasted_iota(jnp.int32, (64, 128), 1)
    energies = jnp.sum(jnp.where(row == lane, tile, 0.0), axis=0, keepdims=True)
    for place in range(16):
        shares_ref[place, :4, :] = tile[4 * place : 4 * place + 4]
        shares_ref[place, 4:5, :] = energies
        shares_ref[place, 5:, :] = jnp.zeros((3, 128), jnp.float32)


def near_kernel(itself_ref, own_ref, three_ref, one_ref, two_ref, out_ref, high_ref, low_ref):
    for offset, ref in enumerate((own_ref, one_ref, two_ref, three_ref)):
        high, low = split(ref[...].reshape(128, 1024))
        high_ref[member_index() ^ offset] = high
        low_ref[member_index() ^ offset] = low

    def both(a):
        return jnp.concatenate([high_ref[a], low_ref[a]], axis=0)

    left = jnp.concatenate([high_ref[0], high_ref[1], low_ref[0], low_ref[1]], axis=0)
    passes = dot(left, jnp.concatenate([high_ref[2], high_ref[3]], axis=0))
    across = dot(left[:256], jnp.concatenate([low_ref[2], low_ref[3]], axis=0)) + passes[256:] + passes[:256]
    products = {(0, 1): four_passes(dot(both(0), both(1))), (2, 3): four_passes(dot(both(2), both(3)))}
    for a in range(2):
        for b in range(2):
            products[a, b + 2] = across[128 * a : 128 * a + 128, 128 * b : 128 * b + 128]
    for place, pair in enumerate(PAIRS):
        tile = complex_tile(products[pair])
        for to in range(16):
            out_ref[to, 4 * place : 4 * place + 4, :] = tile[4 * to : 4 * to + 4]
    out_ref[:, 24:, :] = itself_ref[...]


def total_of(ref):
    total = ref[0]
    for place in range(1, ref.shape[0]):
        total = total + ref[place]
    return total


def sum_kernel(spread_ref, out_ref, itself_ref):
    total = total_of(spread_ref)
    itself_ref[...] = total[24:]
    energies = total[28:29]
    for to in range(4):
        for k in range(1, 4):
            at = 4 * PAIRS.index((min(to, to ^ k), max(to, to ^ k)))
            out_ref[to, 4 * k - 4 : 4 * k, :] = total[at : at + 4]
        out_ref[to, 12:13, :] = energies
        out_ref[to, 13:, :] = jnp.zeros((3, 128), jnp.float32)


def far_kernel(near_ref, own_ref, far_ref, out_ref):
    side = lax.axis_index("z1")
    far = jnp.concatenate(split(far_ref[...].reshape(128, 2048)), axis=0)
    products = four_passes(dot(own_ref[...], far))
    here = complex_tile(products)
    there = complex_tile(products.T)
    energies = near_ref[member_index(), 12:13, :]
    for quarter in range(4):
        same = 4 * side + quarter
        other = 4 * (1 - side) + quarter
        out_ref[same, :16, :] = here[16 * quarter : 16 * quarter + 16]
        out_ref[other, :16, :] = there[16 * quarter : 16 * quarter + 16]
        out_ref[same, 16:, :] = jnp.zeros((8, 128), jnp.float32)
        out_ref[other, 16:17, :] = energies
        out_ref[other, 17:, :] = jnp.zeros((7, 128), jnp.float32)


def pack_kernel(near_ref, itself_ref, far_ref, out_ref):
    far = total_of(far_ref)[:16]
    near = total_of(near_ref)
    tiles = [itself_ref[:4, :]] + [near[4 * k - 4 : 4 * k] for k in range(1, 4)]
    tiles = [modulus(tile) for tile in tiles]
    first = jnp.concatenate(tiles[:2], axis=1)
    second = jnp.concatenate(tiles[2:], axis=1)
    for place in range(16):
        out_ref[place, :16, :] = far
        out_ref[place, 16:20, :] = first
        out_ref[place, 20:, :] = second


def final_kernel(near_ref, far_ref, shares_ref, out_ref):
    energies = [near_ref[member_index() ^ k, 12:13, :64] for k in range(4)]
    energies.append(total_of(far_ref)[16:17, :64] * 0.25)
    columns = [1.0 / jnp.sqrt(energy + EPSILON) for energy in energies]
    diagonal = lax.broadcasted_iota(jnp.int32, (64, 64), 0) == lax.broadcasted_iota(jnp.int32, (64, 64), 1)
    rows = jnp.sum(jnp.where(diagonal, columns[0], 0.0), axis=1, keepdims=True)
    for k in range(5):
        if k < 4:
            at, lane = 16 + 4 * (k // 2), 64 * (k % 2)
            tile = [shares_ref[place, at : at + 4, lane : lane + 64] for place in range(16)]
            tile = jnp.concatenate(tile, axis=0)
            if k > 0:
                tile = jnp.where(is_second(k), tile.T, tile)
        else:
            far = [sum(shares_ref[4 * y + quarter, :16, :] for y in range(4)) for quarter in range(4)]
            tile = modulus(jnp.concatenate(far, axis=0))
        out_ref[k] = tile * rows * columns[k]


def swapped(value, offset):
    pairs = [(source, source ^ offset) for source in range(4)]
    return lax.ppermute(value, QUAD, pairs)


def local(templates):
    templates = pltpu.with_memory_space_constraint(templates, pltpu.HBM)
    first, third = cut(templates, ("half", 0), ("quarter", 3))
    passing = lax.ppermute(first, ("z1", "z0"), [(1, 2), (2, 1)])
    three = swapped(third, 3)
    third, templates = lax.optimization_barrier((third, templates))
    other, mine = cut(templates, ("quarter", 2), ("quarter", 0))
    two = swapped(other, 2)
    other, templates = lax.optimization_barrier((other, templates))
    nearest, second = cut(templates, ("quarter", 1), ("half", 1))
    blocks = [mine, three, swapped(nearest, 1), two]
    second, templates = lax.optimization_barrier((second, templates))
    own, shares = call(own_kernel, (jax.ShapeDtypeStruct((256, 2048), jnp.bfloat16), f32(16, 8, 128)), templates)
    second, passing, own = lax.optimization_barrier((second, passing, own))
    outgoing = choose(second, passing)
    onward = lax.ppermute(outgoing, ("z1", "z0"), [(0, 2), (3, 1), (2, 3), (1, 0)])

    blocks, own, outgoing = lax.optimization_barrier((blocks, own, outgoing))
    cost = pl.CostEstimate(flops=46 * 10**9, bytes_accessed=4 * 2**20, transcendentals=0)
    terms = (pltpu.VMEM((4, 128, 1024), jnp.bfloat16),) * 2
    spread = call(near_kernel, f32(16, 32, 128), shares, *blocks, cost=cost, scratch=terms)
    spread = lax.all_to_all(spread, BAND, 0, 0)
    to_quad, itself = call(sum_kernel, (f32(4, 16, 128), f32(8, 128)), spread)
    near = lax.all_to_all(to_quad, QUAD, 0, 0)
    near, own = lax.optimization_barrier((near, own))
    far = lax.all_to_all(call(far_kernel, f32(8, 24, 128), near, own, onward), FAR, 0, 0)
    shares = lax.all_to_all(call(pack_kernel, f32(16, 24, 128), near, itself, far), BAND, 0, 0)
    return call(final_kernel, f32(5, 64, 64), near, far, shares).transpose(1, 0, 2)


def solution(mesh):
    devices = mesh.devices.reshape(4, 2, 2, 4, 2, 2, 2)
    finer = Mesh(devices, ("y", "x_lo", "core", "z_hi", "z1", "z0", "x_hi"))
    in_specs = (P(None, TMPL, BAND),)
    out_specs = P(TMPL, None, None)
    return jax.shard_map(local, mesh=finer, in_specs=in_specs, out_specs=out_specs, check_vma=False)
```

```python
import functools

import jax
import jax.numpy as jnp
from jax import lax
from jax.experimental import pallas as pl
from jax.experimental.pallas import tpu as pltpu
from jax.sharding import Mesh, PartitionSpec as P

BAND = ("y", "x_lo", "core")
QUAD = ("z0", "x_hi")
FAR = ("z1", "x_lo", "core")
TMPL = ("z_hi", "z1", "z0", "x_hi")
SCALE = 2.0**30
EPSILON = 1e-06 * 2.0**60
VMEM = pl.BlockSpec(memory_space=pltpu.VMEM)
HBM = pl.BlockSpec(memory_space=pltpu.HBM)


def call(kernel, shapes, *args, cost=None, scratch=()):
    return pl.pallas_call(
        kernel,
        scratch_shapes=scratch,
        cost_estimate=cost,
        out_shape=shapes,
        in_specs=[VMEM] * len(args),
        out_specs=jax.tree.map(lambda _: VMEM, shapes),
        compiler_params=pltpu.CompilerParams(vmem_limit_bytes=16 * 2**20),
    )(*args)


def f32(*shape):
    return jax.ShapeDtypeStruct(shape, jnp.float32)


def split(value):
    scaled = value * SCALE
    high = scaled.astype(jnp.bfloat16)
    low = (scaled - high.astype(jnp.float32)).astype(jnp.bfloat16)
    return high, low


def dot(left, right):
    return lax.dot_general(left, right, (((1,), (1,)), ((), ())), preferred_element_type=jnp.float32)


def four_passes(passes):
    return passes[:128, :128] + (passes[:128, 128:] + passes[128:, :128]) + passes[128:, 128:]


def complex_tile(products):
    lane = lax.broadcasted_iota(jnp.int32, (64, 128), 1)
    crossed = pltpu.roll(products[64:], 64, axis=1)
    return products[:64] + jnp.where(lane < 64, crossed, -crossed)


def modulus(tile):
    real_part = jnp.abs(tile[:, :64])
    imag_part = jnp.abs(tile[:, 64:])
    large = jnp.maximum(real_part, imag_part)
    small = jnp.minimum(real_part, imag_part)
    ratio = small / jnp.where(large > 0, large, 1.0)
    return large * jnp.sqrt(1.0 + ratio * ratio)


def member_index():
    return 2 * lax.axis_index("z0") + lax.axis_index("x_hi")


def is_middle():
    return lax.axis_index("z1") != lax.axis_index("z0")


def cut_kernel(pieces, templates_ref, *refs):
    copies = []
    for place, (kind, which) in enumerate(pieces):
        if kind == "half":
            source = templates_ref.at[:, :, 2048 * which : 2048 * which + 2048]
        else:
            at = pl.multiple_of((member_index() ^ which) * 1024, 1024)
            source = templates_ref.at[:, :, pl.ds(at, 1024)]
        copies.append(pltpu.make_async_copy(source, refs[place], refs[-1].at[place]))
    for copy in copies:
        copy.start()
    for copy in copies:
        copy.wait()


def cut(templates, *pieces):
    return pl.pallas_call(
        functools.partial(cut_kernel, pieces),
        out_shape=tuple(f32(2, 64, 2048 if kind == "half" else 1024) for kind, _ in pieces),
        in_specs=[HBM],
        out_specs=(VMEM,) * len(pieces),
        scratch_shapes=[pltpu.SemaphoreType.DMA((len(pieces),))],
        compiler_params=pltpu.CompilerParams(vmem_limit_bytes=8 * 2**20),
    )(templates)


def choose_kernel(second_ref, passing_ref, out_ref, sem):
    @pl.when(is_middle())
    def _():
        copy = pltpu.make_async_copy(passing_ref, out_ref, sem)
        copy.start()
        copy.wait()

    @pl.when(jnp.logical_not(is_middle()))
    def _():
        copy = pltpu.make_async_copy(second_ref, out_ref, sem)
        copy.start()
        copy.wait()


def choose(second, passing):
    return pl.pallas_call(
        choose_kernel,
        out_shape=f32(2, 64, 2048),
        in_specs=[VMEM] * 2,
        out_specs=VMEM,
        scratch_shapes=[pltpu.SemaphoreType.DMA],
        compiler_params=pltpu.CompilerParams(vmem_limit_bytes=8 * 2**20),
    )(second, passing)


PAIRS = ((0, 1), (0, 2), (0, 3), (1, 2), (1, 3), (2, 3))


def is_second(k):
    return (member_index() & (1 if k == 1 else 2)) != 0


def own_kernel(templates_ref, own_ref, shares_ref, mine_ref):
    at = pl.multiple_of(jnp.where(is_middle(), 2048, 0), 2048)
    own_ref[...] = jnp.concatenate(split(templates_ref[:, :, pl.ds(at, 2048)].reshape(128, 2048)), axis=0)
    at = pl.multiple_of(member_index() * 1024, 1024)
    mine_ref[...] = jnp.concatenate(split(templates_ref[:, :, pl.ds(at, 1024)].reshape(128, 1024)), axis=0)
    rows = jnp.concatenate(split(templates_ref[...].reshape(128, 4096)), axis=0)
    tile = complex_tile(four_passes(dot(rows, rows)))
    row = lax.broadcasted_iota(jnp.int32, (64, 128), 0)
    lane = lax.broadcasted_iota(jnp.int32, (64, 128), 1)
    energies = jnp.sum(jnp.where(row == lane, tile, 0.0), axis=0, keepdims=True)
    for place in range(16):
        shares_ref[place, :4, :] = tile[4 * place : 4 * place + 4]
        shares_ref[place, 4:5, :] = energies
        shares_ref[place, 5:, :] = jnp.zeros((3, 128), jnp.float32)


def near_kernel(itself_ref, own_ref, three_ref, one_ref, two_ref, out_ref, high_ref, low_ref):
    high_ref[member_index()] = own_ref[:128, :]
    low_ref[member_index()] = own_ref[128:, :]
    for offset, ref in ((1, one_ref), (2, two_ref), (3, three_ref)):
        high, low = split(ref[...].reshape(128, 1024))
        high_ref[member_index() ^ offset] = high
        low_ref[member_index() ^ offset] = low

    def both(a):
        return jnp.concatenate([high_ref[a], low_ref[a]], axis=0)

    left = jnp.concatenate([high_ref[0], high_ref[1], low_ref[0], low_ref[1]], axis=0)
    passes = dot(left, jnp.concatenate([high_ref[2], high_ref[3]], axis=0))
    across = dot(left[:256], jnp.concatenate([low_ref[2], low_ref[3]], axis=0)) + passes[256:] + passes[:256]
    products = {(0, 1): four_passes(dot(both(0), both(1))), (2, 3): four_passes(dot(both(2), both(3)))}
    for a in range(2):
        for b in range(2):
            products[a, b + 2] = across[128 * a : 128 * a + 128, 128 * b : 128 * b + 128]
    for place, pair in enumerate(PAIRS):
        tile = complex_tile(products[pair])
        for to in range(16):
            out_ref[to, 4 * place : 4 * place + 4, :] = tile[4 * to : 4 * to + 4]
    out_ref[:, 24:, :] = itself_ref[...]


def total_of(ref):
    total = ref[0]
    for place in range(1, ref.shape[0]):
        total = total + ref[place]
    return total


def sum_kernel(spread_ref, out_ref, itself_ref):
    total = total_of(spread_ref)
    itself_ref[...] = total[24:]
    energies = total[28:29]
    for to in range(4):
        for k in range(1, 4):
            at = 4 * PAIRS.index((min(to, to ^ k), max(to, to ^ k)))
            out_ref[to, 4 * k - 4 : 4 * k, :] = total[at : at + 4]
        out_ref[to, 12:13, :] = energies
        out_ref[to, 13:, :] = jnp.zeros((3, 128), jnp.float32)


def far_kernel(near_ref, own_ref, far_ref, out_ref):
    side = lax.axis_index("z1")
    far = jnp.concatenate(split(far_ref[...].reshape(128, 2048)), axis=0)
    products = four_passes(dot(own_ref[...], far))
    here = complex_tile(products)
    there = complex_tile(products.T)
    energies = near_ref[member_index(), 12:13, :]
    for quarter in range(4):
        same = 4 * side + quarter
        other = 4 * (1 - side) + quarter
        out_ref[same, :16, :] = here[16 * quarter : 16 * quarter + 16]
        out_ref[other, :16, :] = there[16 * quarter : 16 * quarter + 16]
        out_ref[same, 16:, :] = jnp.zeros((8, 128), jnp.float32)
        out_ref[other, 16:17, :] = energies
        out_ref[other, 17:, :] = jnp.zeros((7, 128), jnp.float32)


def pack_kernel(near_ref, itself_ref, far_ref, out_ref):
    far = total_of(far_ref)[:16]
    near = total_of(near_ref)
    tiles = [itself_ref[:4, :]] + [near[4 * k - 4 : 4 * k] for k in range(1, 4)]
    tiles = [modulus(tile) for tile in tiles]
    first = jnp.concatenate(tiles[:2], axis=1)
    second = jnp.concatenate(tiles[2:], axis=1)
    for place in range(16):
        out_ref[place, :16, :] = far
        out_ref[place, 16:20, :] = first
        out_ref[place, 20:, :] = second


def final_kernel(near_ref, far_ref, shares_ref, out_ref):
    energies = [near_ref[member_index() ^ k, 12:13, :64] for k in range(4)]
    energies.append(total_of(far_ref)[16:17, :64] * 0.25)
    columns = [1.0 / jnp.sqrt(energy + EPSILON) for energy in energies]
    diagonal = lax.broadcasted_iota(jnp.int32, (64, 64), 0) == lax.broadcasted_iota(jnp.int32, (64, 64), 1)
    rows = jnp.sum(jnp.where(diagonal, columns[0], 0.0), axis=1, keepdims=True)
    for k in range(5):
        if k < 4:
            at, lane = 16 + 4 * (k // 2), 64 * (k % 2)
            tile = [shares_ref[place, at : at + 4, lane : lane + 64] for place in range(16)]
            tile = jnp.concatenate(tile, axis=0)
            if k > 0:
                tile = jnp.where(is_second(k), tile.T, tile)
        else:
            far = [sum(shares_ref[4 * y + quarter, :16, :] for y in range(4)) for quarter in range(4)]
            tile = modulus(jnp.concatenate(far, axis=0))
        out_ref[k] = tile * rows * columns[k]


def swapped(value, offset):
    pairs = [(source, source ^ offset) for source in range(4)]
    return lax.ppermute(value, QUAD, pairs)


def local(templates):
    templates = pltpu.with_memory_space_constraint(templates, pltpu.HBM)
    first, third = cut(templates, ("half", 0), ("quarter", 3))
    passing = lax.ppermute(first, ("z1", "z0"), [(1, 2), (2, 1)])
    three = swapped(third, 3)
    third, templates = lax.optimization_barrier((third, templates))
    other, nearest = cut(templates, ("quarter", 2), ("quarter", 1))
    blocks = [three, swapped(nearest, 1), swapped(other, 2)]
    other, templates = lax.optimization_barrier((other, templates))
    (second,) = cut(templates, ("half", 1))
    second, templates = lax.optimization_barrier((second, templates))
    halves = [jax.ShapeDtypeStruct((256, size), jnp.bfloat16) for size in (2048, 1024)]
    own, shares, mine = call(own_kernel, (halves[0], f32(16, 8, 128), halves[1]), templates)
    second, passing, own = lax.optimization_barrier((second, passing, own))
    outgoing = choose(second, passing)
    onward = lax.ppermute(outgoing, ("z1", "z0"), [(0, 2), (3, 1), (2, 3), (1, 0)])

    blocks, own, outgoing = lax.optimization_barrier((blocks, own, outgoing))
    cost = pl.CostEstimate(flops=46 * 10**9, bytes_accessed=4 * 2**20, transcendentals=0)
    terms = (pltpu.VMEM((4, 128, 1024), jnp.bfloat16),) * 2
    spread = call(near_kernel, f32(16, 32, 128), shares, mine, *blocks, cost=cost, scratch=terms)
    spread = lax.all_to_all(spread, BAND, 0, 0)
    to_quad, itself = call(sum_kernel, (f32(4, 16, 128), f32(8, 128)), spread)
    near = lax.all_to_all(to_quad, QUAD, 0, 0)
    near, own = lax.optimization_barrier((near, own))
    far = lax.all_to_all(call(far_kernel, f32(8, 24, 128), near, own, onward), FAR, 0, 0)
    shares = lax.all_to_all(call(pack_kernel, f32(16, 24, 128), near, itself, far), BAND, 0, 0)
    return call(final_kernel, f32(5, 64, 64), near, far, shares).transpose(1, 0, 2)


def solution(mesh):
    devices = mesh.devices.reshape(4, 2, 2, 4, 2, 2, 2)
    finer = Mesh(devices, ("y", "x_lo", "core", "z_hi", "z1", "z0", "x_hi"))
    in_specs = (P(None, TMPL, BAND),)
    out_specs = P(TMPL, None, None)
    return jax.shard_map(local, mesh=finer, in_specs=in_specs, out_specs=out_specs, check_vma=False)
```
